32 devices in a mesh: ply: 2 (over x), tile: 16 (over z, y, core).
Axes of the slice: x: 2, y: 2, z: 4, core: 2. Of those that a mesh axis runs over, the one named last changes fastest.
Arguments:
- strain: float32 [4, 3, 16, 4096], P(None, None, None, 'tile'), may hold values from -6 to 6
- case_ids: int32 [4], replicated, may hold values from 0 to 3, each once
- angle_ids: int32 [48], P('ply'), may hold values from 0 to 3
- stiffening: float32 [48, 16, 4096], P('ply', None, 'tile'), may hold values from 0.5 to 8
- interface: float32 [48, 16, 4096], P('ply', None, 'tile'), may hold values from 0.5 to 4
Outputs:
- adjoint: float32 [4, 48, 16, 4096], P(None, 'ply', None, 'tile')
- through: float32 [48, 16, 4096], P('ply', None, 'tile')
The draws below stay inside these ranges and needn't reach their ends.
Inputs may be any that keep to these rules, and one draw needn't show every extreme that they name: `case_ids`: each of the 4 load states is taken by exactly one load case.
All inputs are finite; a program needn't handle non-finite values.
Results may differ from the reference program's by a relative error of at most 0.0085.
Values sent between devices are 32-bit elements; how exact they have to be, the bound alone decides.
A program may use at most 64 MiB of HBM per device.

```python
import math
import jax
import jax.numpy as jnp
from jax import lax

ROWS = 16
CASES = 4
ITERS = 4
PLIES = 48
COLS = 4096


def touch_ends(result, stream_key, low, top_value):
    shape = result.shape
    index_at = [jax.random.randint(jax.random.fold_in(stream_key, axis), (), 0, shape[axis]) for axis in range(len(shape))]
    result = result.at[tuple(index_at)].set(low)
    longest = shape.index(max(shape))
    index_at[longest] = (index_at[longest] + 1) % shape[longest]
    return result.at[tuple(index_at)].set(top_value)


def shard_levels(rng, shape, pieces, low, top_value):
    level = 1.0
    for dim, parts in pieces:
        steps = jax.random.uniform(jax.random.fold_in(jax.random.fold_in(rng, 6), dim), (parts,), jnp.float32, low / len(pieces), top_value / len(pieces))
        level = level * jnp.repeat(jnp.exp(steps), shape[dim] // parts).reshape((-1,) + (1,) * (len(shape) - 1 - dim))
    return level


def noise(key, shape, width, reach, cuts=(), kind=jnp.bfloat16):
    loudness = shard_levels(key, shape, cuts, -0.22, 0.18) if cuts else 1.0
    values = jax.random.normal(key, shape, jnp.float32) * width * loudness
    return jnp.minimum(jnp.maximum(values, -reach), reach).astype(kind)


def setup_inputs(seed: int = 0) -> dict:
    key_list = jax.random.split(jax.random.key(seed), 6)
    return {
        "strain": noise(key_list[0], (CASES, 3, ROWS, COLS), 1.0, 6.0, ((3, 16),), jnp.float32),
        "case_ids": jax.random.permutation(key_list[1], CASES).astype(jnp.int32),
        "angle_ids": touch_ends(jax.random.randint(key_list[2], (PLIES,), 0, 4), jax.random.fold_in(key_list[2], 1), 0, 3).astype(jnp.int32),
        "stiffening": jnp.clip(jnp.exp(math.log(8.0) - 2.7725887 * jax.random.uniform(key_list[3], (PLIES, ROWS, COLS), jnp.float32) ** shard_levels(key_list[3], (PLIES, ROWS, COLS), ((0, 2), (2, 16)), -0.2, 0.2)), 0.5, 8.0),
        "interface": jnp.clip(jnp.exp(math.log(4.0) - 2.0794415 * jax.random.uniform(key_list[4], (PLIES, ROWS, COLS), jnp.float32) ** shard_levels(key_list[4], (PLIES, ROWS, COLS), ((0, 2), (2, 16)), -0.2, 0.2)), 0.5, 4.0),
    }


relaxation = 2.0 / 3.0
half_root = 0.7071067811865476
fibre_modulus = 1.0
trans_modulus = 0.5
shear_modulus = 0.3
linear_fibre = 0.3
linear_trans = 0.8
square_fibre = 0.5
square_trans = 1.0
square_shear = 0.8
cross_term = -0.35


def ply_tables(angles):
    one_hot = (angles[:, None] == jnp.arange(4, dtype=jnp.int32)[None, :]).astype(jnp.float32)
    ply_cosine = jnp.sum(one_hot * jnp.array([1.0, half_root, half_root, 0.0], jnp.float32)[None, :], axis=1)
    ply_sine = jnp.sum(one_hot * jnp.array([0.0, half_root, -half_root, 1.0], jnp.float32)[None, :], axis=1)
    ply_cosine = ply_cosine.reshape(-1, 1, 1)
    ply_sine = ply_sine.reshape(-1, 1, 1)
    cond_rows = 4.0 * ply_cosine * ply_cosine + ply_sine * ply_sine
    cond_cols = 4.0 * ply_sine * ply_sine + ply_cosine * ply_cosine
    cond_cross = 3.0 * ply_cosine * ply_sine
    return cond_rows, cond_cols, cond_cross, ply_cosine, ply_sine


def tsai_wu(strain_x, strain_y, strain_xy, ply_cosine, ply_sine):
    cos_sq = ply_cosine * ply_cosine
    sin_sq = ply_sine * ply_sine
    mixed = ply_cosine * ply_sine
    fibre_strain = cos_sq * strain_x + sin_sq * strain_y + mixed * strain_xy
    trans_strain = sin_sq * strain_x + cos_sq * strain_y - mixed * strain_xy
    shear_strain = 2.0 * mixed * (strain_y - strain_x) + (cos_sq - sin_sq) * strain_xy
    fibre_stress = fibre_modulus * fibre_strain
    trans_stress = trans_modulus * trans_strain
    shear_stress = shear_modulus * shear_strain
    first = linear_fibre + 2.0 * square_fibre * fibre_stress + 2.0 * cross_term * trans_stress
    second = linear_trans + 2.0 * square_trans * trans_stress + 2.0 * cross_term * fibre_stress
    return first + second + 2.0 * square_shear * shear_stress


def sweep(padded, source, stiffening, coupling_up, coupling_down, cond_rows, cond_cols, cond_cross):
    widths = [(0, 0)] * (padded.ndim - 2) + [(1, 1), (0, 0)]
    framed = jnp.pad(padded, widths)
    centre = framed[..., 1:-1, 1:-1, 1:-1]
    along_rows = framed[..., 1:-1, 2:, 1:-1] + framed[..., 1:-1, :-2, 1:-1]
    along_cols = framed[..., 1:-1, 1:-1, 2:] + framed[..., 1:-1, 1:-1, :-2]
    diagonal_pairs = framed[..., 1:-1, 2:, 2:] + framed[..., 1:-1, :-2, :-2] - framed[..., 1:-1, 2:, :-2] - framed[..., 1:-1, :-2, 2:]
    overhead = framed[..., 2:, 1:-1, 1:-1]
    beneath = framed[..., :-2, 1:-1, 1:-1]
    image = cond_rows * (2.0 * centre - along_rows) + cond_cols * (2.0 * centre - along_cols) - 0.5 * cond_cross * diagonal_pairs
    image = image + coupling_up * (centre - overhead) + coupling_down * (centre - beneath) + stiffening * centre
    diagonal_sum = 2.0 * cond_rows + 2.0 * cond_cols + coupling_up + coupling_down + stiffening
    return centre + relaxation * (source - image) / diagonal_sum


def reference(strain, case_ids, angle_ids, stiffening, interface):
    cond_rows, cond_cols, cond_cross, ply_cosine, ply_sine = ply_tables(angle_ids)
    coupling_down = jnp.concatenate([jnp.zeros_like(interface[:1]), interface[:-1]], axis=0)

    def step_case(summed, case_id):
        components = lax.dynamic_index_in_dim(strain, case_id, 0, keepdims=False)
        source = tsai_wu(components[0], components[1], components[2], ply_cosine, ply_sine)
        adjoint = jnp.zeros(source.shape, jnp.float32)
        for iteration in range(ITERS):
            padded = jnp.pad(adjoint, ((1, 1), (0, 0), (1, 1)))
            adjoint = sweep(padded, source, stiffening, interface, coupling_down, cond_rows, cond_cols, cond_cross)
        return summed + adjoint * source, adjoint

    start = jnp.zeros(interface.shape, jnp.float32)
    summed, adjoint_all = lax.scan(step_case, start, case_ids)
    through = jnp.cumsum(summed, axis=0) / PLIES
    return adjoint_all, through
```

```python
import functools

import jax
import jax.numpy as jnp
from jax import lax
from jax.experimental import pallas as pl
from jax.experimental.pallas import tpu as pltpu
from jax.sharding import PartitionSpec as P

HALO = 3
PAD = 4
LANES = 128
MESH = pl.DeviceIdType.MESH


def wide(row, rows, tiles):
    row = jnp.broadcast_to(row, (rows, LANES))
    return jnp.concatenate([row] * tiles, axis=1)


def kernel(
    groups,
    tiles,
    case_ref,
    angle_ref,
    strain_ref,
    stiff_hbm,
    inter_hbm,
    adjoint_ref,
    through_ref,
    stiff,
    inter,
    coef,
    strain,
    packed_out,
    packed_in,
    first,
    second,
    third,
    total_out,
    total_in,
    local_sem,
    pack_send,
    pack_recv,
    plane_send,
    plane_recv,
    total_send,
    total_recv,
):
    plies, rows, cols = inter_hbm.shape
    cases = strain_ref.shape[0]
    width = cols + LANES
    mine, tile = lax.axis_index("ply"), lax.axis_index("tile")

    def inside(dp, dt):
        p, t = mine + dp, tile + dt
        return (p >= 0) & (p < groups) & (t >= 0) & (t < tiles)

    has_below, has_above = inside(-1, 0), inside(1, 0)
    has_left, has_right = inside(0, -1), inside(0, 1)

    greeted = [(dp, dt) for dp in (-1, 0, 1) for dt in (-1, 0, 1) if (dp, dt) != (0, 0)]
    greeted += [(dp, 0) for dp in range(1 - groups, groups) if abs(dp) > 1]
    greeted = [(dp, dt) for dp, dt in greeted if abs(dp) < groups]

    locals_ = [
        pltpu.make_async_copy(
            inter_hbm, inter.at[pl.ds(PAD, plies), :, pl.ds(0, cols)], local_sem.at[0]
        ),
        pltpu.make_async_copy(
            stiff_hbm, stiff.at[pl.ds(PAD, plies), :, pl.ds(0, cols)], local_sem.at[1]
        ),
    ]
    for copy in locals_:
        copy.start()

    barrier = pltpu.get_barrier_semaphore()
    count = jnp.int32(0)
    for dp, dt in greeted:
        ok = inside(dp, dt)
        count = count + ok.astype(jnp.int32)

        @pl.when(ok)
        def _(dp=dp, dt=dt):
            pl.semaphore_signal(
                barrier, inc=1, device_id=(mine + dp, tile + dt), device_id_type=MESH
            )

    def table(p, carry):
        angle = angle_ref[p]
        cos_sq = jnp.where(angle == 0, 1.0, jnp.where(angle == 3, 0.0, 0.5))
        sin_sq = 1.0 - cos_sq
        mixed = jnp.where(angle == 1, 0.5, jnp.where(angle == 2, -0.5, 0.0))
        values = (
            4.0 * cos_sq + sin_sq,
            4.0 * sin_sq + cos_sq,
            1.5 * mixed,
            0.3 * cos_sq + 0.65 * sin_sq - 0.96 * mixed,
            0.3 * sin_sq + 0.65 * cos_sq + 0.96 * mixed,
            0.48 * (cos_sq - sin_sq) - 0.35 * mixed,
        )
        at = lax.broadcasted_iota(jnp.int32, (8, LANES), 0)
        block = jnp.zeros((8, LANES), jnp.float32)
        for k, value in enumerate(values):
            block = jnp.where(at == k, value, block)
        coef[p + PAD] = block
        return carry

    lax.fori_loop(0, plies, table, 0)

    def plane_copies(dp):
        if dp > 0:
            moves = [
                (inter_hbm.at[pl.ds(plies - PAD, PAD)], inter.at[pl.ds(0, PAD), :, pl.ds(0, cols)]),
                (stiff_hbm.at[pl.ds(plies - HALO, HALO)], stiff.at[pl.ds(1, HALO), :, pl.ds(0, cols)]),
                (coef.at[pl.ds(plies + 1, HALO)], coef.at[pl.ds(1, HALO)]),
            ]
        else:
            moves = [
                (inter_hbm.at[pl.ds(0, HALO)], inter.at[pl.ds(plies + PAD, HALO), :, pl.ds(0, cols)]),
                (stiff_hbm.at[pl.ds(0, HALO)], stiff.at[pl.ds(plies + PAD, HALO), :, pl.ds(0, cols)]),
                (coef.at[pl.ds(PAD, HALO)], coef.at[pl.ds(plies + PAD, HALO)]),
            ]
        side = int(dp > 0)
        return [
            pltpu.make_async_remote_copy(
                src_ref=src,
                dst_ref=dst,
                send_sem=plane_send.at[side, k],
                recv_sem=plane_recv.at[side, k],
                device_id=(mine + dp, tile),
                device_id_type=MESH,
            )
            for k, (src, dst) in enumerate(moves)
        ]

    pl.semaphore_wait(barrier, count)
    for dp in (1, -1):
        if groups > 1:

            @pl.when(inside(dp, 0))
            def _(dp=dp):
                for copy in plane_copies(dp):
                    copy.start()

    lane = lax.broadcasted_iota(jnp.int32, (rows, LANES), 1)
    slot = lane // 4
    low = jnp.zeros((rows, LANES), jnp.float32)
    high = jnp.zeros((rows, LANES), jnp.float32)
    for c in range(cases):
        for k in range(3):
            at = c * 3 + k
            plane = strain_ref[case_ref[c], k]
            strain[at, :, 0:cols] = plane
            head, tail = plane[:, :LANES], plane[:, cols - LANES :]
            low = jnp.where(slot == at, pltpu.roll(head, 4 * at, 1), low)
            high = jnp.where(slot == at, pltpu.roll(tail, 4 * at + 4, 1), high)
    packed_out[0, 2] = low
    packed_out[1, 2] = high

    for copy in locals_:
        copy.wait()

    def pack(p, carry):
        inter_low, inter_high, stiff_low, stiff_high = carry
        here = slot == p
        up, down = 4 * p, 4 * p + 4
        e = p + PAD
        inter_low = jnp.where(here, pltpu.roll(inter[e, :, 0:LANES], up, 1), inter_low)
        inter_high = jnp.where(here, pltpu.roll(inter[e, :, cols - LANES : cols], down, 1), inter_high)
        stiff_low = jnp.where(here, pltpu.roll(stiff[e, :, 0:LANES], up, 1), stiff_low)
        stiff_high = jnp.where(here, pltpu.roll(stiff[e, :, cols - LANES : cols], down, 1), stiff_high)
        return inter_low, inter_high, stiff_low, stiff_high

    zero = jnp.zeros((rows, LANES), jnp.float32)
    inter_low, inter_high, stiff_low, stiff_high = lax.fori_loop(0, plies, pack, (zero,) * 4)
    packed_out[0, 0] = inter_low
    packed_out[1, 0] = inter_high
    packed_out[0, 1] = stiff_low
    packed_out[1, 1] = stiff_high

    def pack_copy(dp, dt):
        depth = 3 if dp == 0 else 2
        group, side = 1 - dp, int(dt < 0)
        return pltpu.make_async_remote_copy(
            src_ref=packed_out.at[1 - side, pl.ds(0, depth)],
            dst_ref=packed_in.at[group, side, pl.ds(0, depth)],
            send_sem=pack_send.at[group, side],
            recv_sem=pack_recv.at[group, side],
            device_id=(mine + dp, tile + dt),
            device_id_type=MESH,
        )

    corners = [(dp, dt) for dp in (0, -1, 1) for dt in (-1, 1) if abs(dp) < groups]
    for dp, dt in corners:

        @pl.when(inside(dp, dt))
        def _(dp=dp, dt=dt):
            pack_copy(dp, dt).start()

    for group in range(3):
        for side, there in ((0, has_left), (1, has_right)):

            @pl.when(jnp.logical_not(there))
            def _(group=group, side=side):
                packed_in[group, side] = jnp.zeros((3, rows, LANES), jnp.float32)

    @pl.when(jnp.logical_not(has_below))
    def _():
        inter[PAD - 1] = jnp.zeros((rows, width), jnp.float32)
        for c in range(cases):
            for field in (first, second, third):
                field[c, PAD - 1] = jnp.zeros((rows, width), jnp.float32)

    @pl.when(jnp.logical_not(has_above))
    def _():
        for c in range(cases):
            for field in (first, second, third):
                field[c, plies + PAD] = jnp.zeros((rows, width), jnp.float32)

    for dp, dt in corners:

        @pl.when(inside(-dp, -dt))
        def _(dp=dp, dt=dt):
            pack_copy(dp, dt).wait_recv()

    for dp in (1, -1):
        if groups > 1:

            @pl.when(inside(-dp, 0))
            def _(dp=dp):
                for copy in plane_copies(dp):
                    copy.wait_recv()

    upper_half = lane < LANES // 2

    def halo_tile(group, kind, q):
        right = pltpu.roll(packed_in[group, 1, kind], lax.rem(LANES - 4 * q, LANES), 1)
        left = pltpu.roll(packed_in[group, 0, kind], LANES - 4 - 4 * q, 1)
        return jnp.where(upper_half, right, left)

    for at in range(3 * cases):
        strain[at, :, cols:width] = halo_tile(1, 2, jnp.int32(at))

    @pl.when(has_below)
    def _():
        inter[0, :, cols:width] = halo_tile(0, 0, jnp.int32(plies - PAD))

    reach = [
        (jnp.where(has_below, k, PAD), jnp.where(has_above, plies + 2 * PAD - k, plies + PAD))
        for k in (1, 2, 3)
    ]

    left_in = jnp.where(has_left, 2.0 / 3.0, 0.0)
    right_in = jnp.where(has_right, 2.0 / 3.0, 0.0)
    numerator = jnp.concatenate(
        [
            jnp.full((rows, cols), 2.0 / 3.0, jnp.float32),
            jnp.where(upper_half, right_in, left_in),
        ],
        axis=1,
    )

    def source_of(e, c, count):
        sx = strain[3 * c, :, 0 : count * LANES]
        sy = strain[3 * c + 1, :, 0 : count * LANES]
        sxy = strain[3 * c + 2, :, 0 : count * LANES]
        a, b, g = (wide(coef[e, k : k + 1, :], rows, count) for k in (3, 4, 5))
        return 1.1 + a * sx + b * sy + g * sxy

    def start(e, carry):
        group = (e + plies - PAD) // plies
        q = e - PAD - (group - 1) * plies
        inter[e, :, cols:width] = halo_tile(group, 0, q)
        rigid = jnp.concatenate([stiff[e, :, 0:cols], halo_tile(group, 1, q)], axis=1)
        weight = numerator / (10.0 + inter[e] + inter[e - 1] + rigid)
        stiff[e] = weight
        for c in range(cases):
            first[c, e] = weight * source_of(e, c, width // LANES)
        return carry

    lax.fori_loop(reach[0][0], reach[0][1], start, 0)

    row = lax.broadcasted_iota(jnp.int32, (rows, width), 0)
    not_top, not_bottom = row < rows - 1, row > 0

    def swept(e, c, field, tables):
        rows_c, cols_c, cross_c, weight, over, under = tables
        v = field[c, e]
        right = pltpu.roll(v, width - 1, 1)
        left = pltpu.roll(v, 1, 1)
        along = rows_c * v
        cross = cross_c * (right - left)
        upper = jnp.where(not_top, pltpu.roll(along + cross, rows - 1, 0), 0.0)
        lower = jnp.where(not_bottom, pltpu.roll(along - cross, 1, 0), 0.0)
        pull = (upper + lower) + cols_c * (right + left)
        pull = pull + (over * field[c, e + 1] + under * field[c, e - 1])
        return (v * (1.0 / 3.0) + first[c, e]) + weight * pull

    def tables_of(e):
        count = width // LANES
        rows_c, cols_c, cross_c = (wide(coef[e, k : k + 1, :], rows, count) for k in range(3))
        return rows_c, cols_c, cross_c, stiff[e], inter[e], inter[e - 1]

    for (begin, end), old, new in ((reach[1], first, second), (reach[2], second, third)):

        def step(e, carry, old=old, new=new):
            tables = tables_of(e)
            for c in range(cases):
                new[c, e] = swept(e, c, old, tables)
            return carry

        lax.fori_loop(begin, end, step, 0)

    share = 1.0 / (plies * groups)

    def last(p, running):
        e = p + PAD
        tables = tables_of(e)
        for c in range(cases):
            value = swept(e, c, third, tables)[:, 0:cols]
            adjoint_ref[c, p] = value
            running = running + value * source_of(e, c, cols // LANES)
        through_ref[p] = running * share
        return running

    running = lax.fori_loop(0, plies, last, jnp.zeros((rows, cols), jnp.float32))
    total_out[...] = running * share

    def total_copy(by):
        return pltpu.make_async_remote_copy(
            src_ref=total_out,
            dst_ref=total_in.at[by - 1],
            send_sem=total_send.at[by - 1],
            recv_sem=total_recv.at[by - 1],
            device_id=(mine + by, tile),
            device_id_type=MESH,
        )

    for by in range(1, groups):

        @pl.when(inside(by, 0))
        def _(by=by):
            total_copy(by).start()

    for dp, dt in corners:

        @pl.when(inside(dp, dt))
        def _(dp=dp, dt=dt):
            pack_copy(dp, dt).wait_send()

    for dp in (1, -1):
        if groups > 1:

            @pl.when(inside(dp, 0))
            def _(dp=dp):
                for copy in plane_copies(dp):
                    copy.wait_send()

    for by in range(1, groups):

        @pl.when(inside(-by, 0))
        def _(by=by):
            total_copy(by).wait_recv()

            def add(p, carry):
                through_ref[p] = through_ref[p] + total_in[by - 1]
                return carry

            lax.fori_loop(0, plies, add, 0)

    for by in range(1, groups):

        @pl.when(inside(by, 0))
        def _(by=by):
            total_copy(by).wait_send()


def body(groups, tiles, strain, case_ids, angle_ids, stiffening, interface):
    plies, rows, cols = interface.shape
    cases = strain.shape[0]
    ext, width = plies + 2 * PAD, cols + LANES
    vmem = lambda *shape: pltpu.VMEM(shape, jnp.float32)
    dma = pltpu.SemaphoreType.DMA
    others = max(groups - 1, 1)
    return pl.pallas_call(
        functools.partial(kernel, groups, tiles),
        out_shape=(
            jax.ShapeDtypeStruct((cases, plies, rows, cols), jnp.float32),
            jax.ShapeDtypeStruct((plies, rows, cols), jnp.float32),
        ),
        in_specs=[
            pl.BlockSpec(memory_space=pltpu.SMEM),
            pl.BlockSpec(memory_space=pltpu.SMEM),
            pl.BlockSpec(memory_space=pltpu.VMEM),
            pl.BlockSpec(memory_space=pl.ANY),
            pl.BlockSpec(memory_space=pl.ANY),
        ],
        out_specs=(
            pl.BlockSpec(memory_space=pltpu.VMEM),
            pl.BlockSpec(memory_space=pltpu.VMEM),
        ),
        scratch_shapes=[
            vmem(ext, rows, width),
            vmem(ext, rows, width),
            vmem(ext, 8, LANES),
            vmem(3 * cases, rows, width),
            vmem(2, 3, rows, LANES),
            vmem(3, 2, 3, rows, LANES),
            vmem(cases, ext, rows, width),
            vmem(cases, ext, rows, width),
            vmem(cases, ext, rows, width),
            vmem(rows, cols),
            vmem(others, rows, cols),
            dma((2,)),
            dma((3, 2)),
            dma((3, 2)),
            dma((2, 3)),
            dma((2, 3)),
            dma((others,)),
            dma((others,)),
        ],
        compiler_params=pltpu.CompilerParams(
            collective_id=0, has_side_effects=True, vmem_limit_bytes=40 * 1024 * 1024
        ),
    )(case_ids, angle_ids, strain, stiffening, interface)


def solution(mesh):
    return jax.shard_map(
        functools.partial(body, mesh.shape["ply"], mesh.shape["tile"]),
        mesh=mesh,
        in_specs=(
            P(None, None, None, "tile"),
            P(),
            P("ply"),
            P("ply", None, "tile"),
            P("ply", None, "tile"),
        ),
        out_specs=(P(None, "ply", None, "tile"), P("ply", None, "tile")),
        check_vma=False,
    )
```

```python
import functools

import jax
import jax.numpy as jnp
from jax import lax
from jax.experimental import pallas as pl
from jax.experimental.pallas import tpu as pltpu
from jax.sharding import PartitionSpec as P

HALO = 3
PAD = 4
LANES = 128
MESH = pl.DeviceIdType.MESH


def wide(row, rows, tiles):
    row = jnp.broadcast_to(row, (rows, LANES))
    return jnp.concatenate([row] * tiles, axis=1)


def kernel(
    groups,
    tiles,
    case_hbm,
    angle_hbm,
    strain_hbm,
    stiff_hbm,
    inter_hbm,
    adjoint_ref,
    through_ref,
    case_ref,
    angle_ref,
    strain_ref,
    stiff,
    inter,
    coef,
    strain,
    packed_out,
    packed_in,
    first,
    second,
    third,
    total_out,
    total_in,
    local_sem,
    pack_send,
    pack_recv,
    plane_send,
    plane_recv,
    total_send,
    total_recv,
):
    plies, rows, cols = inter_hbm.shape
    cases = strain_hbm.shape[0]
    width = cols + LANES
    mine, tile = lax.axis_index("ply"), lax.axis_index("tile")

    def inside(dp, dt):
        p, t = mine + dp, tile + dt
        return (p >= 0) & (p < groups) & (t >= 0) & (t < tiles)

    has_below, has_above = inside(-1, 0), inside(1, 0)
    has_left, has_right = inside(0, -1), inside(0, 1)

    greeted = [(dp, dt) for dp in (-1, 0, 1) for dt in (-1, 0, 1) if (dp, dt) != (0, 0)]
    greeted += [(dp, 0) for dp in range(1 - groups, groups) if abs(dp) > 1]
    greeted = [(dp, dt) for dp, dt in greeted if abs(dp) < groups]

    locals_ = [
        pltpu.make_async_copy(angle_hbm, angle_ref, local_sem.at[2]),
        pltpu.make_async_copy(case_hbm, case_ref, local_sem.at[3]),
        pltpu.make_async_copy(strain_hbm, strain_ref, local_sem.at[4]),
        pltpu.make_async_copy(
            inter_hbm, inter.at[pl.ds(PAD, plies), :, pl.ds(0, cols)], local_sem.at[0]
        ),
        pltpu.make_async_copy(
            stiff_hbm, stiff.at[pl.ds(PAD, plies), :, pl.ds(0, cols)], local_sem.at[1]
        ),
    ]
    for copy in locals_:
        copy.start()

    barrier = pltpu.get_barrier_semaphore()
    count = jnp.int32(0)
    for dp, dt in greeted:
        ok = inside(dp, dt)
        count = count + ok.astype(jnp.int32)

        @pl.when(ok)
        def _(dp=dp, dt=dt):
            pl.semaphore_signal(
                barrier, inc=1, device_id=(mine + dp, tile + dt), device_id_type=MESH
            )

    for copy in locals_[:2]:
        copy.wait()

    def table(p, carry):
        angle = angle_ref[p]
        cos_sq = jnp.where(angle == 0, 1.0, jnp.where(angle == 3, 0.0, 0.5))
        sin_sq = 1.0 - cos_sq
        mixed = jnp.where(angle == 1, 0.5, jnp.where(angle == 2, -0.5, 0.0))
        values = (
            4.0 * cos_sq + sin_sq,
            4.0 * sin_sq + cos_sq,
            1.5 * mixed,
            0.3 * cos_sq + 0.65 * sin_sq - 0.96 * mixed,
            0.3 * sin_sq + 0.65 * cos_sq + 0.96 * mixed,
            0.48 * (cos_sq - sin_sq) - 0.35 * mixed,
        )
        at = lax.broadcasted_iota(jnp.int32, (8, LANES), 0)
        block = jnp.zeros((8, LANES), jnp.float32)
        for k, value in enumerate(values):
            block = jnp.where(at == k, value, block)
        coef[p + PAD] = block
        return carry

    lax.fori_loop(0, plies, table, 0, unroll=4)

    def plane_copies(dp):
        if dp > 0:
            moves = [
                (inter_hbm.at[pl.ds(plies - PAD, PAD)], inter.at[pl.ds(0, PAD), :, pl.ds(0, cols)]),
                (stiff_hbm.at[pl.ds(plies - HALO, HALO)], stiff.at[pl.ds(1, HALO), :, pl.ds(0, cols)]),
                (coef.at[pl.ds(plies + 1, HALO)], coef.at[pl.ds(1, HALO)]),
            ]
        else:
            moves = [
                (inter_hbm.at[pl.ds(0, HALO)], inter.at[pl.ds(plies + PAD, HALO), :, pl.ds(0, cols)]),
                (stiff_hbm.at[pl.ds(0, HALO)], stiff.at[pl.ds(plies + PAD, HALO), :, pl.ds(0, cols)]),
                (coef.at[pl.ds(PAD, HALO)], coef.at[pl.ds(plies + PAD, HALO)]),
            ]
        side = int(dp > 0)
        return [
            pltpu.make_async_remote_copy(
                src_ref=src,
                dst_ref=dst,
                send_sem=plane_send.at[side, k],
                recv_sem=plane_recv.at[side, k],
                device_id=(mine + dp, tile),
                device_id_type=MESH,
            )
            for k, (src, dst) in enumerate(moves)
        ]

    pl.semaphore_wait(barrier, count)
    for dp in (1, -1):
        if groups > 1:

            @pl.when(inside(dp, 0))
            def _(dp=dp):
                for copy in plane_copies(dp):
                    copy.start()

    lane = lax.broadcasted_iota(jnp.int32, (rows, LANES), 1)
    slot = lane // 4
    locals_[2].wait()
    low = jnp.zeros((rows, LANES), jnp.float32)
    high = jnp.zeros((rows, LANES), jnp.float32)
    for c in range(cases):
        for k in range(3):
            at = c * 3 + k
            plane = strain_ref[case_ref[c], k]
            strain[at, :, 0:cols] = plane
            head, tail = plane[:, :LANES], plane[:, cols - LANES :]
            low = jnp.where(slot == at, pltpu.roll(head, 4 * at, 1), low)
            high = jnp.where(slot == at, pltpu.roll(tail, 4 * at + 4, 1), high)
    packed_out[0, 2] = low
    packed_out[1, 2] = high

    for copy in locals_[3:]:
        copy.wait()

    def pack(p, carry):
        inter_low, inter_high, stiff_low, stiff_high = carry
        here = slot == p
        up, down = 4 * p, 4 * p + 4
        e = p + PAD
        inter_low = jnp.where(here, pltpu.roll(inter[e, :, 0:LANES], up, 1), inter_low)
        inter_high = jnp.where(here, pltpu.roll(inter[e, :, cols - LANES : cols], down, 1), inter_high)
        stiff_low = jnp.where(here, pltpu.roll(stiff[e, :, 0:LANES], up, 1), stiff_low)
        stiff_high = jnp.where(here, pltpu.roll(stiff[e, :, cols - LANES : cols], down, 1), stiff_high)
        return inter_low, inter_high, stiff_low, stiff_high

    zero = jnp.zeros((rows, LANES), jnp.float32)
    inter_low, inter_high, stiff_low, stiff_high = lax.fori_loop(0, plies, pack, (zero,) * 4, unroll=8)
    packed_out[0, 0] = inter_low
    packed_out[1, 0] = inter_high
    packed_out[0, 1] = stiff_low
    packed_out[1, 1] = stiff_high

    def pack_copy(dp, dt):
        depth = 3 if dp == 0 else 2
        group, side = 1 - dp, int(dt < 0)
        return pltpu.make_async_remote_copy(
            src_ref=packed_out.at[1 - side, pl.ds(0, depth)],
            dst_ref=packed_in.at[group, side, pl.ds(0, depth)],
            send_sem=pack_send.at[group, side],
            recv_sem=pack_recv.at[group, side],
            device_id=(mine + dp, tile + dt),
            device_id_type=MESH,
        )

    corners = [(dp, dt) for dp in (0, -1, 1) for dt in (-1, 1) if abs(dp) < groups]
    for dp, dt in corners:

        @pl.when(inside(dp, dt))
        def _(dp=dp, dt=dt):
            pack_copy(dp, dt).start()

    def source_of(e, c, begin, count):
        at = pl.ds(begin * LANES, count * LANES)
        sx, sy, sxy = (strain[3 * c + k, :, at] for k in range(3))
        a, b, g = (wide(coef[e, k : k + 1, :], rows, count) for k in (3, 4, 5))
        return 1.1 + a * sx + b * sy + g * sxy

    full = cols // LANES

    def start_block(e):
        rigid = inter[e, :, 0:cols] + inter[e - 1, :, 0:cols] + stiff[e, :, 0:cols]
        weight = (2.0 / 3.0) / (10.0 + rigid)
        stiff[e, :, 0:cols] = weight
        for c in range(cases):
            first[c, e, :, 0:cols] = weight * source_of(e, c, 0, full)

    def start_own(e, carry):
        start_block(e)
        return carry

    lax.fori_loop(PAD + 1, PAD + plies, start_own, 0, unroll=1)

    for group in range(3):
        for side, there in ((0, has_left), (1, has_right)):

            @pl.when(jnp.logical_not(there))
            def _(group=group, side=side):
                packed_in[group, side] = jnp.zeros((3, rows, LANES), jnp.float32)

    @pl.when(jnp.logical_not(has_below))
    def _():
        inter[PAD - 1] = jnp.zeros((rows, width), jnp.float32)
        for c in range(cases):
            for field in (first, second, third):
                field[c, PAD - 1] = jnp.zeros((rows, width), jnp.float32)

    @pl.when(jnp.logical_not(has_above))
    def _():
        for c in range(cases):
            for field in (first, second, third):
                field[c, plies + PAD] = jnp.zeros((rows, width), jnp.float32)

    for dp, dt in corners:

        @pl.when(inside(-dp, -dt))
        def _(dp=dp, dt=dt):
            pack_copy(dp, dt).wait_recv()

    for dp in (1, -1):
        if groups > 1:

            @pl.when(inside(-dp, 0))
            def _(dp=dp):
                for copy in plane_copies(dp):
                    copy.wait_recv()

    upper_half = lane < LANES // 2

    def halo_tile(group, kind, q):
        right = pltpu.roll(packed_in[group, 1, kind], lax.rem(LANES - 4 * q, LANES), 1)
        left = pltpu.roll(packed_in[group, 0, kind], LANES - 4 - 4 * q, 1)
        return jnp.where(upper_half, right, left)

    for at in range(3 * cases):
        strain[at, :, cols:width] = halo_tile(1, 2, jnp.int32(at))

    start_block(PAD)

    numerator = jnp.where(
        upper_half, jnp.where(has_right, 2.0 / 3.0, 0.0), jnp.where(has_left, 2.0 / 3.0, 0.0)
    )

    def start_halo(e, group, q, under):
        over = halo_tile(group, 0, q)
        inter[e, :, cols:width] = over
        weight = numerator / (10.0 + over + under + halo_tile(group, 1, q))
        stiff[e, :, cols:width] = weight
        for c in range(cases):
            first[c, e, :, cols:width] = weight * source_of(e, c, full, 1)
        return over

    @pl.when(has_below)
    def _():
        under = halo_tile(0, 0, jnp.int32(plies - PAD))
        inter[0, :, cols:width] = under

        def below(e, under):
            start_block(e)
            return start_halo(e, 0, plies - PAD + e, under)

        under = lax.fori_loop(1, PAD, below, under)

    under = jnp.where(has_below, inter[PAD - 1, :, cols:width], 0.0)
    under = lax.fori_loop(
        0, plies, lambda p, under: start_halo(p + PAD, 1, p, under), under, unroll=4
    )

    @pl.when(has_above)
    def _():
        def above(q, under):
            start_block(q + plies + PAD)
            return start_halo(q + plies + PAD, 2, q, under)

        lax.fori_loop(0, HALO, above, under)

    half = rows // 2
    row = lax.broadcasted_iota(jnp.int32, (half, width), 0)
    is_last, is_first = row == half - 1, row == 0

    def from_next_row(x):
        a, b = (pltpu.roll(part, half - 1, 0) for part in (x[:half], x[half:]))
        return jnp.concatenate([jnp.where(is_last, b, a), jnp.where(is_last, 0.0, b)], axis=0)

    def from_row_before(x):
        a, b = (pltpu.roll(part, 1, 0) for part in (x[:half], x[half:]))
        return jnp.concatenate([jnp.where(is_first, 0.0, a), jnp.where(is_first, a, b)], axis=0)

    def swept(e, c, field, tables):
        rows_c, cols_c, cross_c, weight, over, under = tables
        v = field[c, e]
        right = pltpu.roll(v, width - 1, 1)
        left = pltpu.roll(v, 1, 1)
        along = rows_c * v
        cross = cross_c * (right - left)
        upper = from_next_row(along + cross)
        lower = from_row_before(along - cross)
        pull = (upper + lower) + cols_c * (right + left)
        pull = pull + (over * field[c, e + 1] + under * field[c, e - 1])
        return (v * (1.0 / 3.0) + first[c, e]) + weight * pull

    def tables_of(e):
        count = width // LANES
        rows_c, cols_c, cross_c = (wide(coef[e, k : k + 1, :], rows, count) for k in range(3))
        return rows_c, cols_c, cross_c, stiff[e], inter[e], inter[e - 1]

    for depth, old, new in ((2, first, second), (1, second, third)):

        def step(e, carry, old=old, new=new):
            tables = tables_of(e)
            for c in range(cases):
                new[c, e] = swept(e, c, old, tables)
            return carry

        @pl.when(has_below)
        def _(depth=depth, step=step):
            lax.fori_loop(PAD - depth, PAD, step, 0)

        @pl.when(has_above)
        def _(depth=depth, step=step):
            lax.fori_loop(plies + PAD, plies + PAD + depth, step, 0)

        lax.fori_loop(PAD, plies + PAD, step, 0, unroll=2)

    share = 1.0 / (plies * groups)

    def last(p, running):
        e = p + PAD
        tables = tables_of(e)
        for c in range(cases):
            value = swept(e, c, third, tables)[:, 0:cols]
            adjoint_ref[c, p] = value
            running = running + value * source_of(e, c, 0, full)
        through_ref[p] = running * share
        return running

    running = lax.fori_loop(0, plies, last, jnp.zeros((rows, cols), jnp.float32), unroll=2)
    total_out[...] = running * share

    def total_copy(by):
        return pltpu.make_async_remote_copy(
            src_ref=total_out,
            dst_ref=total_in.at[by - 1],
            send_sem=total_send.at[by - 1],
            recv_sem=total_recv.at[by - 1],
            device_id=(mine + by, tile),
            device_id_type=MESH,
        )

    for by in range(1, groups):

        @pl.when(inside(by, 0))
        def _(by=by):
            total_copy(by).start()

    for dp, dt in corners:

        @pl.when(inside(dp, dt))
        def _(dp=dp, dt=dt):
            pack_copy(dp, dt).wait_send()

    for dp in (1, -1):
        if groups > 1:

            @pl.when(inside(dp, 0))
            def _(dp=dp):
                for copy in plane_copies(dp):
                    copy.wait_send()

    for by in range(1, groups):

        @pl.when(inside(-by, 0))
        def _(by=by):
            total_copy(by).wait_recv()

            def add(p, carry):
                through_ref[p] = through_ref[p] + total_in[by - 1]
                return carry

            lax.fori_loop(0, plies, add, 0, unroll=4)

    for by in range(1, groups):

        @pl.when(inside(by, 0))
        def _(by=by):
            total_copy(by).wait_send()


def body(groups, tiles, strain, case_ids, angle_ids, stiffening, interface):
    plies, rows, cols = interface.shape
    cases = strain.shape[0]
    ext, width = plies + 2 * PAD, cols + LANES
    vmem = lambda *shape: pltpu.VMEM(shape, jnp.float32)
    dma = pltpu.SemaphoreType.DMA
    others = max(groups - 1, 1)
    return pl.pallas_call(
        functools.partial(kernel, groups, tiles),
        out_shape=(
            jax.ShapeDtypeStruct((cases, plies, rows, cols), jnp.float32),
            jax.ShapeDtypeStruct((plies, rows, cols), jnp.float32),
        ),
        in_specs=[pl.BlockSpec(memory_space=pltpu.HBM)] * 5,
        out_specs=(
            pl.BlockSpec(memory_space=pltpu.VMEM),
            pl.BlockSpec(memory_space=pltpu.VMEM),
        ),
        scratch_shapes=[
            pltpu.SMEM(case_ids.shape, jnp.int32),
            pltpu.SMEM(angle_ids.shape, jnp.int32),
            vmem(*strain.shape),
            vmem(ext, rows, width),
            vmem(ext, rows, width),
            vmem(ext, 8, LANES),
            vmem(3 * cases, rows, width),
            vmem(2, 3, rows, LANES),
            vmem(3, 2, 3, rows, LANES),
            vmem(cases, ext, rows, width),
            vmem(cases, ext, rows, width),
            vmem(cases, ext, rows, width),
            vmem(rows, cols),
            vmem(others, rows, cols),
            dma((5,)),
            dma((3, 2)),
            dma((3, 2)),
            dma((2, 3)),
            dma((2, 3)),
            dma((others,)),
            dma((others,)),
        ],
        compiler_params=pltpu.CompilerParams(
            collective_id=0, has_side_effects=True, vmem_limit_bytes=40 * 1024 * 1024
        ),
    )(case_ids, angle_ids, strain, stiffening, interface)


def solution(mesh):
    return jax.shard_map(
        functools.partial(body, mesh.shape["ply"], mesh.shape["tile"]),
        mesh=mesh,
        in_specs=(
            P(None, None, None, "tile"),
            P(),
            P("ply"),
            P("ply", None, "tile"),
            P("ply", None, "tile"),
        ),
        out_specs=(P(None, "ply", None, "tile"), P("ply", None, "tile")),
        check_vma=False,
    )
```

```python
import functools

import jax
import jax.numpy as jnp
from jax import lax
from jax.experimental import pallas as pl
from jax.experimental.pallas import tpu as pltpu
from jax.sharding import PartitionSpec as P

HALO = 3
PAD = 4
LANES = 128
MESH = pl.DeviceIdType.MESH


def wide(row, rows, tiles):
    row = jnp.broadcast_to(row, (rows, LANES))
    return jnp.concatenate([row] * tiles, axis=1)


def kernel(
    groups,
    tiles,
    case_hbm,
    angle_hbm,
    strain_hbm,
    stiff_hbm,
    inter_hbm,
    adjoint_hbm,
    through_ref,
    case_ref,
    angle_ref,
    strain_ref,
    stiff,
    inter,
    coef,
    strain,
    packed_out,
    packed_in,
    first,
    second,
    third,
    adjoint_ref,
    total_out,
    total_in,
    local_sem,
    result_sem,
    pack_send,
    pack_recv,
    plane_send,
    plane_recv,
    total_send,
    total_recv,
):
    plies, rows, cols = inter_hbm.shape
    cases = strain_hbm.shape[0]
    width = cols + LANES
    mine, tile = lax.axis_index("ply"), lax.axis_index("tile")

    def inside(dp, dt):
        p, t = mine + dp, tile + dt
        return (p >= 0) & (p < groups) & (t >= 0) & (t < tiles)

    has_below, has_above = inside(-1, 0), inside(1, 0)
    has_left, has_right = inside(0, -1), inside(0, 1)

    greeted = [(dp, dt) for dp in (-1, 0, 1) for dt in (-1, 0, 1) if (dp, dt) != (0, 0)]
    greeted += [(dp, 0) for dp in range(1 - groups, groups) if abs(dp) > 1]
    greeted = [(dp, dt) for dp, dt in greeted if abs(dp) < groups]

    locals_ = [
        pltpu.make_async_copy(angle_hbm, angle_ref, local_sem.at[2]),
        pltpu.make_async_copy(case_hbm, case_ref, local_sem.at[3]),
        pltpu.make_async_copy(strain_hbm, strain_ref, local_sem.at[4]),
        pltpu.make_async_copy(
            inter_hbm, inter.at[pl.ds(PAD, plies), :, pl.ds(0, cols)], local_sem.at[0]
        ),
        pltpu.make_async_copy(
            stiff_hbm, stiff.at[pl.ds(PAD, plies), :, pl.ds(0, cols)], local_sem.at[1]
        ),
    ]
    for copy in locals_:
        copy.start()

    barrier = pltpu.get_barrier_semaphore()
    count = jnp.int32(0)
    for dp, dt in greeted:
        ok = inside(dp, dt)
        count = count + ok.astype(jnp.int32)

        @pl.when(ok)
        def _(dp=dp, dt=dt):
            pl.semaphore_signal(
                barrier, inc=1, device_id=(mine + dp, tile + dt), device_id_type=MESH
            )

    for copy in locals_[:2]:
        copy.wait()

    def table(p, carry):
        angle = angle_ref[p]
        cos_sq = jnp.where(angle == 0, 1.0, jnp.where(angle == 3, 0.0, 0.5))
        sin_sq = 1.0 - cos_sq
        mixed = jnp.where(angle == 1, 0.5, jnp.where(angle == 2, -0.5, 0.0))
        values = (
            4.0 * cos_sq + sin_sq,
            4.0 * sin_sq + cos_sq,
            1.5 * mixed,
            0.3 * cos_sq + 0.65 * sin_sq - 0.96 * mixed,
            0.3 * sin_sq + 0.65 * cos_sq + 0.96 * mixed,
            0.48 * (cos_sq - sin_sq) - 0.35 * mixed,
        )
        at = lax.broadcasted_iota(jnp.int32, (8, LANES), 0)
        block = jnp.zeros((8, LANES), jnp.float32)
        for k, value in enumerate(values):
            block = jnp.where(at == k, value, block)
        coef[p + PAD] = block
        return carry

    lax.fori_loop(0, plies, table, 0, unroll=4)

    def plane_copies(dp):
        if dp > 0:
            moves = [
                (inter_hbm.at[pl.ds(plies - PAD, PAD)], inter.at[pl.ds(0, PAD), :, pl.ds(0, cols)]),
                (stiff_hbm.at[pl.ds(plies - HALO, HALO)], stiff.at[pl.ds(1, HALO), :, pl.ds(0, cols)]),
                (coef.at[pl.ds(plies + 1, HALO)], coef.at[pl.ds(1, HALO)]),
            ]
        else:
            moves = [
                (inter_hbm.at[pl.ds(0, HALO)], inter.at[pl.ds(plies + PAD, HALO), :, pl.ds(0, cols)]),
                (stiff_hbm.at[pl.ds(0, HALO)], stiff.at[pl.ds(plies + PAD, HALO), :, pl.ds(0, cols)]),
                (coef.at[pl.ds(PAD, HALO)], coef.at[pl.ds(plies + PAD, HALO)]),
            ]
        side = int(dp > 0)
        return [
            pltpu.make_async_remote_copy(
                src_ref=src,
                dst_ref=dst,
                send_sem=plane_send.at[side, k],
                recv_sem=plane_recv.at[side, k],
                device_id=(mine + dp, tile),
                device_id_type=MESH,
            )
            for k, (src, dst) in enumerate(moves)
        ]

    pl.semaphore_wait(barrier, count)
    for dp in (1, -1):
        if groups > 1:

            @pl.when(inside(dp, 0))
            def _(dp=dp):
                for copy in plane_copies(dp):
                    copy.start()

    lane = lax.broadcasted_iota(jnp.int32, (rows, LANES), 1)
    slot = lane // 4
    locals_[2].wait()
    low = jnp.zeros((rows, LANES), jnp.float32)
    high = jnp.zeros((rows, LANES), jnp.float32)
    for c in range(cases):
        for k in range(3):
            at = c * 3 + k
            plane = strain_ref[case_ref[c], k]
            strain[at, :, 0:cols] = plane
            head, tail = plane[:, :LANES], plane[:, cols - LANES :]
            low = jnp.where(slot == at, pltpu.roll(head, 4 * at, 1), low)
            high = jnp.where(slot == at, pltpu.roll(tail, 4 * at + 4, 1), high)
    packed_out[0, 2] = low
    packed_out[1, 2] = high

    for copy in locals_[3:]:
        copy.wait()

    def pack(p, carry):
        inter_low, inter_high, stiff_low, stiff_high = carry
        here = slot == p
        up, down = 4 * p, 4 * p + 4
        e = p + PAD
        inter_low = jnp.where(here, pltpu.roll(inter[e, :, 0:LANES], up, 1), inter_low)
        inter_high = jnp.where(here, pltpu.roll(inter[e, :, cols - LANES : cols], down, 1), inter_high)
        stiff_low = jnp.where(here, pltpu.roll(stiff[e, :, 0:LANES], up, 1), stiff_low)
        stiff_high = jnp.where(here, pltpu.roll(stiff[e, :, cols - LANES : cols], down, 1), stiff_high)
        return inter_low, inter_high, stiff_low, stiff_high

    zero = jnp.zeros((rows, LANES), jnp.float32)
    inter_low, inter_high, stiff_low, stiff_high = lax.fori_loop(0, plies, pack, (zero,) * 4, unroll=8)
    packed_out[0, 0] = inter_low
    packed_out[1, 0] = inter_high
    packed_out[0, 1] = stiff_low
    packed_out[1, 1] = stiff_high

    def pack_copy(dp, dt):
        depth = 3 if dp == 0 else 2
        group, side = 1 - dp, int(dt < 0)
        return pltpu.make_async_remote_copy(
            src_ref=packed_out.at[1 - side, pl.ds(0, depth)],
            dst_ref=packed_in.at[group, side, pl.ds(0, depth)],
            send_sem=pack_send.at[group, side],
            recv_sem=pack_recv.at[group, side],
            device_id=(mine + dp, tile + dt),
            device_id_type=MESH,
        )

    corners = [(dp, dt) for dp in (0, -1, 1) for dt in (-1, 1) if abs(dp) < groups]
    for dp, dt in corners:

        @pl.when(inside(dp, dt))
        def _(dp=dp, dt=dt):
            pack_copy(dp, dt).start()

    def source_of(e, c, begin, count):
        at = pl.ds(begin * LANES, count * LANES)
        sx, sy, sxy = (strain[3 * c + k, :, at] for k in range(3))
        a, b, g = (wide(coef[e, k : k + 1, :], rows, count) for k in (3, 4, 5))
        return 1.1 + a * sx + b * sy + g * sxy

    full = cols // LANES

    def start_block(e):
        rigid = inter[e, :, 0:cols] + inter[e - 1, :, 0:cols] + stiff[e, :, 0:cols]
        weight = (2.0 / 3.0) / (10.0 + rigid)
        stiff[e, :, 0:cols] = weight
        for c in range(cases):
            first[c, e, :, 0:cols] = weight * source_of(e, c, 0, full)

    def start_pair(i, carry):
        for k in range(2):
            start_block(PAD + 1 + 2 * i + k)
        return carry

    lax.fori_loop(0, (plies - 1) // 2, start_pair, 0)
    if plies % 2 == 0:
        start_block(PAD + plies - 1)

    for group in range(3):
        for side, there in ((0, has_left), (1, has_right)):

            @pl.when(jnp.logical_not(there))
            def _(group=group, side=side):
                packed_in[group, side] = jnp.zeros((3, rows, LANES), jnp.float32)

    @pl.when(jnp.logical_not(has_below))
    def _():
        inter[PAD - 1] = jnp.zeros((rows, width), jnp.float32)
        for c in range(cases):
            for field in (first, second, third):
                field[c, PAD - 1] = jnp.zeros((rows, width), jnp.float32)

    @pl.when(jnp.logical_not(has_above))
    def _():
        for c in range(cases):
            for field in (first, second, third):
                field[c, plies + PAD] = jnp.zeros((rows, width), jnp.float32)

    for dp, dt in corners:

        @pl.when(inside(-dp, -dt))
        def _(dp=dp, dt=dt):
            pack_copy(dp, dt).wait_recv()

    for dp in (1, -1):
        if groups > 1:

            @pl.when(inside(-dp, 0))
            def _(dp=dp):
                for copy in plane_copies(dp):
                    copy.wait_recv()

    upper_half = lane < LANES // 2

    def halo_tile(group, kind, q):
        right = pltpu.roll(packed_in[group, 1, kind], lax.rem(LANES - 4 * q, LANES), 1)
        left = pltpu.roll(packed_in[group, 0, kind], LANES - 4 - 4 * q, 1)
        return jnp.where(upper_half, right, left)

    for at in range(3 * cases):
        strain[at, :, cols:width] = halo_tile(1, 2, jnp.int32(at))

    start_block(PAD)

    numerator = jnp.where(
        upper_half, jnp.where(has_right, 2.0 / 3.0, 0.0), jnp.where(has_left, 2.0 / 3.0, 0.0)
    )

    def start_halo(e, group, q, under):
        over = halo_tile(group, 0, q)
        inter[e, :, cols:width] = over
        weight = numerator / (10.0 + over + under + halo_tile(group, 1, q))
        stiff[e, :, cols:width] = weight
        for c in range(cases):
            first[c, e, :, cols:width] = weight * source_of(e, c, full, 1)
        return over

    @pl.when(has_below)
    def _():
        under = halo_tile(0, 0, jnp.int32(plies - PAD))
        inter[0, :, cols:width] = under

        def below(e, under):
            start_block(e)
            return start_halo(e, 0, plies - PAD + e, under)

        under = lax.fori_loop(1, PAD, below, under)

    under = jnp.where(has_below, inter[PAD - 1, :, cols:width], 0.0)
    under = lax.fori_loop(
        0, plies, lambda p, under: start_halo(p + PAD, 1, p, under), under, unroll=4
    )

    @pl.when(has_above)
    def _():
        def above(q, under):
            start_block(q + plies + PAD)
            return start_halo(q + plies + PAD, 2, q, under)

        lax.fori_loop(0, HALO, above, under)

    half = rows // 2
    row = lax.broadcasted_iota(jnp.int32, (half, width), 0)
    is_last, is_first = row == half - 1, row == 0

    def from_next_row(x):
        a, b = (pltpu.roll(part, half - 1, 0) for part in (x[:half], x[half:]))
        return jnp.concatenate([jnp.where(is_last, b, a), jnp.where(is_last, 0.0, b)], axis=0)

    def from_row_before(x):
        a, b = (pltpu.roll(part, 1, 0) for part in (x[:half], x[half:]))
        return jnp.concatenate([jnp.where(is_first, 0.0, a), jnp.where(is_first, a, b)], axis=0)

    def swept(e, c, field, tables):
        rows_c, cols_c, cross_c, weight, over, under = tables
        v = field[c, e]
        right = pltpu.roll(v, width - 1, 1)
        left = pltpu.roll(v, 1, 1)
        along = rows_c * v
        cross = cross_c * (right - left)
        upper = from_next_row(along + cross)
        lower = from_row_before(along - cross)
        pull = (upper + lower) + cols_c * (right + left)
        pull = pull + (over * field[c, e + 1] + under * field[c, e - 1])
        return (v * (1.0 / 3.0) + first[c, e]) + weight * pull

    def tables_of(e):
        count = width // LANES
        rows_c, cols_c, cross_c = (wide(coef[e, k : k + 1, :], rows, count) for k in range(3))
        return rows_c, cols_c, cross_c, stiff[e], inter[e], inter[e - 1]

    for depth, old, new in ((2, first, second), (1, second, third)):

        def step(e, carry, old=old, new=new):
            tables = tables_of(e)
            for c in range(cases):
                new[c, e] = swept(e, c, old, tables)
            return carry

        @pl.when(has_below)
        def _(depth=depth, step=step):
            lax.fori_loop(PAD - depth, PAD, step, 0)

        @pl.when(has_above)
        def _(depth=depth, step=step):
            lax.fori_loop(plies + PAD, plies + PAD + depth, step, 0)

        lax.fori_loop(PAD, plies + PAD, step, 0, unroll=2)

    share = 1.0 / (plies * groups)

    def last(p, running):
        e = p + PAD
        tables = tables_of(e)
        for c in range(cases):
            value = swept(e, c, third, tables)[:, 0:cols]
            adjoint_ref[c, p] = value
            running = running + value * source_of(e, c, 0, full)
        through_ref[p] = running * share
        pltpu.make_async_copy(
            adjoint_ref.at[:, pl.ds(p, 1)], adjoint_hbm.at[:, pl.ds(p, 1)], result_sem.at[0]
        ).start()
        return running

    running = lax.fori_loop(0, plies, last, jnp.zeros((rows, cols), jnp.float32), unroll=2)
    total_out[...] = running * share

    def total_copy(by):
        return pltpu.make_async_remote_copy(
            src_ref=total_out,
            dst_ref=total_in.at[by - 1],
            send_sem=total_send.at[by - 1],
            recv_sem=total_recv.at[by - 1],
            device_id=(mine + by, tile),
            device_id_type=MESH,
        )

    for by in range(1, groups):

        @pl.when(inside(by, 0))
        def _(by=by):
            total_copy(by).start()

    for dp, dt in corners:

        @pl.when(inside(dp, dt))
        def _(dp=dp, dt=dt):
            pack_copy(dp, dt).wait_send()

    for dp in (1, -1):
        if groups > 1:

            @pl.when(inside(dp, 0))
            def _(dp=dp):
                for copy in plane_copies(dp):
                    copy.wait_send()

    for by in range(1, groups):

        @pl.when(inside(-by, 0))
        def _(by=by):
            total_copy(by).wait_recv()

            def add(p, carry):
                through_ref[p] = through_ref[p] + total_in[by - 1]
                return carry

            lax.fori_loop(0, plies, add, 0, unroll=4)

    for by in range(1, groups):

        @pl.when(inside(by, 0))
        def _(by=by):
            total_copy(by).wait_send()

    pltpu.make_async_copy(adjoint_ref, adjoint_hbm, result_sem.at[0]).wait()


def body(groups, tiles, strain, case_ids, angle_ids, stiffening, interface):
    plies, rows, cols = interface.shape
    cases = strain.shape[0]
    ext, width = plies + 2 * PAD, cols + LANES
    vmem = lambda *shape: pltpu.VMEM(shape, jnp.float32)
    dma = pltpu.SemaphoreType.DMA
    others = max(groups - 1, 1)
    return pl.pallas_call(
        functools.partial(kernel, groups, tiles),
        out_shape=(
            jax.ShapeDtypeStruct((cases, plies, rows, cols), jnp.float32),
            jax.ShapeDtypeStruct((plies, rows, cols), jnp.float32),
        ),
        in_specs=[pl.BlockSpec(memory_space=pltpu.HBM)] * 5,
        out_specs=(
            pl.BlockSpec(memory_space=pltpu.HBM),
            pl.BlockSpec(memory_space=pltpu.VMEM),
        ),
        scratch_shapes=[
            pltpu.SMEM(case_ids.shape, jnp.int32),
            pltpu.SMEM(angle_ids.shape, jnp.int32),
            vmem(*strain.shape),
            vmem(ext, rows, width),
            vmem(ext, rows, width),
            vmem(ext, 8, LANES),
            vmem(3 * cases, rows, width),
            vmem(2, 3, rows, LANES),
            vmem(3, 2, 3, rows, LANES),
            vmem(cases, ext, rows, width),
            vmem(cases, ext, rows, width),
            vmem(cases, ext, rows, width),
            vmem(cases, plies, rows, cols),
            vmem(rows, cols),
            vmem(others, rows, cols),
            dma((5,)),
            dma((1,)),
            dma((3, 2)),
            dma((3, 2)),
            dma((2, 3)),
            dma((2, 3)),
            dma((others,)),
            dma((others,)),
        ],
        compiler_params=pltpu.CompilerParams(
            collective_id=0, has_side_effects=True, vmem_limit_bytes=56 * 1024 * 1024
        ),
    )(case_ids, angle_ids, strain, stiffening, interface)


def solution(mesh):
    return jax.shard_map(
        functools.partial(body, mesh.shape["ply"], mesh.shape["tile"]),
        mesh=mesh,
        in_specs=(
            P(None, None, None, "tile"),
            P(),
            P("ply"),
            P("ply", None, "tile"),
            P("ply", None, "tile"),
        ),
        out_specs=(P(None, "ply", None, "tile"), P("ply", None, "tile")),
        check_vma=False,
    )
```

```python
import functools

import jax
import jax.numpy as jnp
from jax import lax
from jax.experimental import pallas as pl
from jax.experimental.pallas import tpu as pltpu
from jax.sharding import PartitionSpec as P

HALO = 3
PAD = 4
LANES = 128
MESH = pl.DeviceIdType.MESH


def wide(row, rows, tiles):
    row = jnp.broadcast_to(row, (rows, LANES))
    return jnp.concatenate([row] * tiles, axis=1)


def kernel(
    groups,
    tiles,
    case_hbm,
    angle_hbm,
    strain_hbm,
    stiff_hbm,
    inter_hbm,
    adjoint_hbm,
    through_ref,
    case_ref,
    angle_ref,
    strain_ref,
    stiff,
    inter,
    coef,
    strain,
    packed_out,
    packed_in,
    first,
    second,
    third,
    adjoint_ref,
    total_out,
    total_in,
    local_sem,
    result_sem,
    pack_send,
    pack_recv,
    plane_send,
    plane_recv,
    total_send,
    total_recv,
):
    plies, rows, cols = inter_hbm.shape
    cases = strain_hbm.shape[0]
    width = cols + LANES
    mine, tile = lax.axis_index("ply"), lax.axis_index("tile")

    def inside(dp, dt):
        p, t = mine + dp, tile + dt
        return (p >= 0) & (p < groups) & (t >= 0) & (t < tiles)

    has_below, has_above = inside(-1, 0), inside(1, 0)
    has_left, has_right = inside(0, -1), inside(0, 1)

    greeted = [(dp, dt) for dp in (-1, 0, 1) for dt in (-1, 0, 1) if (dp, dt) != (0, 0)]
    greeted += [(dp, 0) for dp in range(1 - groups, groups) if abs(dp) > 1]
    greeted = [(dp, dt) for dp, dt in greeted if abs(dp) < groups]

    locals_ = [
        pltpu.make_async_copy(angle_hbm, angle_ref, local_sem.at[2]),
        pltpu.make_async_copy(case_hbm, case_ref, local_sem.at[3]),
        pltpu.make_async_copy(strain_hbm, strain_ref, local_sem.at[4]),
        pltpu.make_async_copy(
            inter_hbm, inter.at[pl.ds(PAD, plies), :, pl.ds(0, cols)], local_sem.at[0]
        ),
        pltpu.make_async_copy(
            stiff_hbm, stiff.at[pl.ds(PAD, plies), :, pl.ds(0, cols)], local_sem.at[1]
        ),
    ]
    for copy in locals_:
        copy.start()

    barrier = pltpu.get_barrier_semaphore()
    count = jnp.int32(0)
    for dp, dt in greeted:
        ok = inside(dp, dt)
        count = count + ok.astype(jnp.int32)

        @pl.when(ok)
        def _(dp=dp, dt=dt):
            pl.semaphore_signal(
                barrier, inc=1, device_id=(mine + dp, tile + dt), device_id_type=MESH
            )

    for copy in locals_[:2]:
        copy.wait()

    def table(p, carry):
        angle = angle_ref[p]
        cos_sq = jnp.where(angle == 0, 1.0, jnp.where(angle == 3, 0.0, 0.5))
        sin_sq = 1.0 - cos_sq
        mixed = jnp.where(angle == 1, 0.5, jnp.where(angle == 2, -0.5, 0.0))
        values = (
            4.0 * cos_sq + sin_sq,
            4.0 * sin_sq + cos_sq,
            1.5 * mixed,
            0.3 * cos_sq + 0.65 * sin_sq - 0.96 * mixed,
            0.3 * sin_sq + 0.65 * cos_sq + 0.96 * mixed,
            0.48 * (cos_sq - sin_sq) - 0.35 * mixed,
        )
        at = lax.broadcasted_iota(jnp.int32, (8, LANES), 0)
        block = jnp.zeros((8, LANES), jnp.float32)
        for k, value in enumerate(values):
            block = jnp.where(at == k, value, block)
        coef[p + PAD] = block
        return carry

    lax.fori_loop(0, plies, table, 0, unroll=4)

    def plane_copies(dp):
        if dp > 0:
            moves = [
                (inter_hbm.at[pl.ds(plies - PAD, PAD)], inter.at[pl.ds(0, PAD), :, pl.ds(0, cols)]),
                (stiff_hbm.at[pl.ds(plies - HALO, HALO)], stiff.at[pl.ds(1, HALO), :, pl.ds(0, cols)]),
                (coef.at[pl.ds(plies + 1, HALO)], coef.at[pl.ds(1, HALO)]),
            ]
        else:
            moves = [
                (inter_hbm.at[pl.ds(0, HALO)], inter.at[pl.ds(plies + PAD, HALO), :, pl.ds(0, cols)]),
                (stiff_hbm.at[pl.ds(0, HALO)], stiff.at[pl.ds(plies + PAD, HALO), :, pl.ds(0, cols)]),
                (coef.at[pl.ds(PAD, HALO)], coef.at[pl.ds(plies + PAD, HALO)]),
            ]
        side = int(dp > 0)
        return [
            pltpu.make_async_remote_copy(
                src_ref=src,
                dst_ref=dst,
                send_sem=plane_send.at[side, k],
                recv_sem=plane_recv.at[side, k],
                device_id=(mine + dp, tile),
                device_id_type=MESH,
            )
            for k, (src, dst) in enumerate(moves)
        ]

    pl.semaphore_wait(barrier, count)
    for dp in (1, -1):
        if groups > 1:

            @pl.when(inside(dp, 0))
            def _(dp=dp):
                for copy in plane_copies(dp):
                    copy.start()

    lane = lax.broadcasted_iota(jnp.int32, (rows, LANES), 1)
    slot = lane // 4
    locals_[2].wait()
    low = jnp.zeros((rows, LANES), jnp.float32)
    high = jnp.zeros((rows, LANES), jnp.float32)
    for c in range(cases):
        for k in range(3):
            at = c * 3 + k
            plane = strain_ref[case_ref[c], k]
            strain[at, :, 0:cols] = plane
            head, tail = plane[:, :LANES], plane[:, cols - LANES :]
            low = jnp.where(slot == at, pltpu.roll(head, 4 * at, 1), low)
            high = jnp.where(slot == at, pltpu.roll(tail, 4 * at + 4, 1), high)
    packed_out[0, 2] = low
    packed_out[1, 2] = high

    for copy in locals_[3:]:
        copy.wait()

    def pack(p, carry):
        inter_low, inter_high, stiff_low, stiff_high = carry
        here = slot == p
        up, down = 4 * p, 4 * p + 4
        e = p + PAD
        inter_low = jnp.where(here, pltpu.roll(inter[e, :, 0:LANES], up, 1), inter_low)
        inter_high = jnp.where(here, pltpu.roll(inter[e, :, cols - LANES : cols], down, 1), inter_high)
        stiff_low = jnp.where(here, pltpu.roll(stiff[e, :, 0:LANES], up, 1), stiff_low)
        stiff_high = jnp.where(here, pltpu.roll(stiff[e, :, cols - LANES : cols], down, 1), stiff_high)
        return inter_low, inter_high, stiff_low, stiff_high

    zero = jnp.zeros((rows, LANES), jnp.float32)
    inter_low, inter_high, stiff_low, stiff_high = lax.fori_loop(0, plies, pack, (zero,) * 4, unroll=8)
    packed_out[0, 0] = inter_low
    packed_out[1, 0] = inter_high
    packed_out[0, 1] = stiff_low
    packed_out[1, 1] = stiff_high

    def pack_copy(dp, dt):
        depth = 3 if dp == 0 else 2
        group, side = 1 - dp, int(dt < 0)
        return pltpu.make_async_remote_copy(
            src_ref=packed_out.at[1 - side, pl.ds(0, depth)],
            dst_ref=packed_in.at[group, side, pl.ds(0, depth)],
            send_sem=pack_send.at[group, side],
            recv_sem=pack_recv.at[group, side],
            device_id=(mine + dp, tile + dt),
            device_id_type=MESH,
        )

    corners = [(dp, dt) for dp in (0, -1, 1) for dt in (-1, 1) if abs(dp) < groups]
    for dp, dt in corners:

        @pl.when(inside(dp, dt))
        def _(dp=dp, dt=dt):
            pack_copy(dp, dt).start()

    def source_of(e, c, begin, count):
        at = pl.ds(begin * LANES, count * LANES)
        sx, sy, sxy = (strain[3 * c + k, :, at] for k in range(3))
        a, b, g = (wide(coef[e, k : k + 1, :], rows, count) for k in (3, 4, 5))
        return 1.1 + a * sx + b * sy + g * sxy

    full = cols // LANES

    def start_block(e):
        rigid = inter[e, :, 0:cols] + inter[e - 1, :, 0:cols] + stiff[e, :, 0:cols]
        weight = (2.0 / 3.0) / (10.0 + rigid)
        stiff[e, :, 0:cols] = weight
        for c in range(cases):
            first[c, e, :, 0:cols] = weight * source_of(e, c, 0, full)

    def start_pair(i, carry):
        for k in range(2):
            start_block(PAD + 1 + 2 * i + k)
        return carry

    lax.fori_loop(0, (plies - 1) // 2, start_pair, 0)
    if plies % 2 == 0:
        start_block(PAD + plies - 1)

    for group in range(3):
        for side, there in ((0, has_left), (1, has_right)):

            @pl.when(jnp.logical_not(there))
            def _(group=group, side=side):
                packed_in[group, side] = jnp.zeros((3, rows, LANES), jnp.float32)

    @pl.when(jnp.logical_not(has_below))
    def _():
        inter[PAD - 1] = jnp.zeros((rows, width), jnp.float32)
        for c in range(cases):
            for field in (first, second, third):
                field[c, PAD - 1] = jnp.zeros((rows, width), jnp.float32)

    @pl.when(jnp.logical_not(has_above))
    def _():
        for c in range(cases):
            for field in (first, second, third):
                field[c, plies + PAD] = jnp.zeros((rows, width), jnp.float32)

    for dp, dt in corners:

        @pl.when(inside(-dp, -dt))
        def _(dp=dp, dt=dt):
            pack_copy(dp, dt).wait_recv()

    for dp in (1, -1):
        if groups > 1:

            @pl.when(inside(-dp, 0))
            def _(dp=dp):
                for copy in plane_copies(dp):
                    copy.wait_recv()

    upper_half = lane < LANES // 2

    def halo_tile(group, kind, q):
        right = pltpu.roll(packed_in[group, 1, kind], lax.rem(LANES - 4 * q, LANES), 1)
        left = pltpu.roll(packed_in[group, 0, kind], LANES - 4 - 4 * q, 1)
        return jnp.where(upper_half, right, left)

    for at in range(3 * cases):
        strain[at, :, cols:width] = halo_tile(1, 2, jnp.int32(at))

    start_block(PAD)

    numerator = jnp.where(
        upper_half, jnp.where(has_right, 2.0 / 3.0, 0.0), jnp.where(has_left, 2.0 / 3.0, 0.0)
    )

    def start_halo(e, group, q, under):
        over = halo_tile(group, 0, q)
        inter[e, :, cols:width] = over
        weight = numerator / (10.0 + over + under + halo_tile(group, 1, q))
        stiff[e, :, cols:width] = weight
        for c in range(cases):
            first[c, e, :, cols:width] = weight * source_of(e, c, full, 1)
        return over

    @pl.when(has_below)
    def _():
        under = halo_tile(0, 0, jnp.int32(plies - PAD))
        inter[0, :, cols:width] = under

        def below(e, under):
            start_block(e)
            return start_halo(e, 0, plies - PAD + e, under)

        under = lax.fori_loop(1, PAD, below, under)

    under = jnp.where(has_below, inter[PAD - 1, :, cols:width], 0.0)
    under = lax.fori_loop(
        0, plies, lambda p, under: start_halo(p + PAD, 1, p, under), under, unroll=4
    )

    @pl.when(has_above)
    def _():
        def above(q, under):
            start_block(q + plies + PAD)
            return start_halo(q + plies + PAD, 2, q, under)

        lax.fori_loop(0, HALO, above, under)

    half = rows // 2
    row = lax.broadcasted_iota(jnp.int32, (half, width), 0)
    is_last, is_first = row == half - 1, row == 0

    def from_next_row(x):
        a, b = (pltpu.roll(part, half - 1, 0) for part in (x[:half], x[half:]))
        return jnp.concatenate([jnp.where(is_last, b, a), jnp.where(is_last, 0.0, b)], axis=0)

    def from_row_before(x):
        a, b = (pltpu.roll(part, 1, 0) for part in (x[:half], x[half:]))
        return jnp.concatenate([jnp.where(is_first, 0.0, a), jnp.where(is_first, a, b)], axis=0)

    def swept(e, c, field, tables):
        rows_c, cols_c, cross_c, weight, over, under = tables
        v = field[c, e]
        right = pltpu.roll(v, width - 1, 1)
        left = pltpu.roll(v, 1, 1)
        along = rows_c * v
        cross = cross_c * (right - left)
        upper = from_next_row(along + cross)
        lower = from_row_before(along - cross)
        pull = (upper + lower) + cols_c * (right + left)
        pull = pull + (over * field[c, e + 1] + under * field[c, e - 1])
        return (v * (1.0 / 3.0) + first[c, e]) + weight * pull

    def tables_of(e):
        count = width // LANES
        rows_c, cols_c, cross_c = (wide(coef[e, k : k + 1, :], rows, count) for k in range(3))
        return rows_c, cols_c, cross_c, stiff[e], inter[e], inter[e - 1]

    for depth, old, new in ((2, first, second), (1, second, third)):

        def step(e, carry, old=old, new=new):
            tables = tables_of(e)
            for c in range(cases):
                new[c, e] = swept(e, c, old, tables)
            return carry

        @pl.when(has_below)
        def _(depth=depth, step=step):
            lax.fori_loop(PAD - depth, PAD, step, 0)

        @pl.when(has_above)
        def _(depth=depth, step=step):
            lax.fori_loop(plies + PAD, plies + PAD + depth, step, 0)

        lax.fori_loop(PAD, plies + PAD, step, 0, unroll=2)

    share = 1.0 / (plies * groups)

    def last(p, running):
        e = p + PAD
        tables = tables_of(e)
        for c in range(cases):
            value = swept(e, c, third, tables)[:, 0:cols]
            adjoint_ref[c, p] = value
            running = running + value * source_of(e, c, 0, full)
        through_ref[p] = running * share
        pltpu.make_async_copy(
            adjoint_ref.at[:, pl.ds(p, 1)], adjoint_hbm.at[:, pl.ds(p, 1)], result_sem.at[0]
        ).start()
        return running

    running = lax.fori_loop(0, plies, last, jnp.zeros((rows, cols), jnp.float32), unroll=2)
    total_out[...] = running * share

    def total_copy(by):
        return pltpu.make_async_remote_copy(
            src_ref=total_out,
            dst_ref=total_in.at[by - 1],
            send_sem=total_send.at[by - 1],
            recv_sem=total_recv.at[by - 1],
            device_id=(mine + by, tile),
            device_id_type=MESH,
        )

    for by in range(1, groups):

        @pl.when(inside(by, 0))
        def _(by=by):
            total_copy(by).start()

    for dp, dt in corners:

        @pl.when(inside(dp, dt))
        def _(dp=dp, dt=dt):
            pack_copy(dp, dt).wait_send()

    for dp in (1, -1):
        if groups > 1:

            @pl.when(inside(dp, 0))
            def _(dp=dp):
                for copy in plane_copies(dp):
                    copy.wait_send()

    for by in range(1, groups):

        @pl.when(inside(-by, 0))
        def _(by=by):
            total_copy(by).wait_recv()

            def add(p, carry):
                through_ref[p] = through_ref[p] + total_in[by - 1]
                return carry

            lax.fori_loop(0, plies, add, 0, unroll=4)

    for by in range(1, groups):

        @pl.when(inside(by, 0))
        def _(by=by):
            total_copy(by).wait_send()

    pltpu.make_async_copy(adjoint_ref, adjoint_hbm, result_sem.at[0]).wait()


def hand_over(parts, adjoint_in, through_in, adjoint_out, through_out, sem):
    plies = through_in.shape[0]
    step = plies // parts
    copies = []
    for k in range(parts):
        at = pl.ds(k * step, step)
        for c in range(adjoint_in.shape[0]):
            copies.append((adjoint_in.at[c, at], adjoint_out.at[c, at]))
        copies.append((through_in.at[at], through_out.at[at]))
    copies = [pltpu.make_async_copy(a, b, sem.at[k]) for k, (a, b) in enumerate(copies)]
    for copy in copies:
        copy.start()
    for copy in copies:
        copy.wait()


def handed_over(adjoint, through):
    parts = 2 if through.shape[0] % 2 == 0 else 1
    hbm = pl.BlockSpec(memory_space=pltpu.HBM)
    return pl.pallas_call(
        functools.partial(hand_over, parts),
        out_shape=tuple(jax.ShapeDtypeStruct(a.shape, a.dtype) for a in (adjoint, through)),
        in_specs=[hbm, hbm],
        out_specs=(hbm, hbm),
        scratch_shapes=[pltpu.SemaphoreType.DMA((parts * (adjoint.shape[0] + 1),))],
        compiler_params=pltpu.CompilerParams(vmem_limit_bytes=56 * 1024 * 1024),
    )(adjoint, through)


def body(groups, tiles, strain, case_ids, angle_ids, stiffening, interface):
    plies, rows, cols = interface.shape
    cases = strain.shape[0]
    ext, width = plies + 2 * PAD, cols + LANES
    vmem = lambda *shape: pltpu.VMEM(shape, jnp.float32)
    dma = pltpu.SemaphoreType.DMA
    others = max(groups - 1, 1)
    adjoint, through = pl.pallas_call(
        functools.partial(kernel, groups, tiles),
        out_shape=(
            jax.ShapeDtypeStruct((cases, plies, rows, cols), jnp.float32),
            jax.ShapeDtypeStruct((plies, rows, cols), jnp.float32),
        ),
        in_specs=[pl.BlockSpec(memory_space=pltpu.HBM)] * 5,
        out_specs=(
            pl.BlockSpec(memory_space=pltpu.HBM),
            pl.BlockSpec(memory_space=pltpu.VMEM),
        ),
        scratch_shapes=[
            pltpu.SMEM(case_ids.shape, jnp.int32),
            pltpu.SMEM(angle_ids.shape, jnp.int32),
            vmem(*strain.shape),
            vmem(ext, rows, width),
            vmem(ext, rows, width),
            vmem(ext, 8, LANES),
            vmem(3 * cases, rows, width),
            vmem(2, 3, rows, LANES),
            vmem(3, 2, 3, rows, LANES),
            vmem(cases, ext, rows, width),
            vmem(cases, ext, rows, width),
            vmem(cases, ext, rows, width),
            vmem(cases, plies, rows, cols),
            vmem(rows, cols),
            vmem(others, rows, cols),
            dma((5,)),
            dma((1,)),
            dma((3, 2)),
            dma((3, 2)),
            dma((2, 3)),
            dma((2, 3)),
            dma((others,)),
            dma((others,)),
        ],
        compiler_params=pltpu.CompilerParams(
            collective_id=0, has_side_effects=True, vmem_limit_bytes=56 * 1024 * 1024
        ),
    )(case_ids, angle_ids, strain, stiffening, interface)
    return tuple(handed_over(adjoint, through))


def solution(mesh):
    return jax.shard_map(
        functools.partial(body, mesh.shape["ply"], mesh.shape["tile"]),
        mesh=mesh,
        in_specs=(
            P(None, None, None, "tile"),
            P(),
            P("ply"),
            P("ply", None, "tile"),
            P("ply", None, "tile"),
        ),
        out_specs=(P(None, "ply", None, "tile"), P("ply", None, "tile")),
        check_vma=False,
    )
```

```python
import functools

import jax
import jax.numpy as jnp
from jax import lax
from jax.experimental import pallas as pl
from jax.experimental.pallas import tpu as pltpu
from jax.sharding import PartitionSpec as P

HALO = 3
PAD = 4
LANES = 128
MESH = pl.DeviceIdType.MESH


def wide(row, rows, tiles):
    row = jnp.broadcast_to(row, (rows, LANES))
    return jnp.concatenate([row] * tiles, axis=1)


def kernel(
    groups,
    tiles,
    case_hbm,
    angle_hbm,
    strain_hbm,
    stiff_hbm,
    inter_hbm,
    adjoint_hbm,
    through_ref,
    case_ref,
    angle_ref,
    strain_ref,
    stiff,
    inter,
    coef,
    strain,
    packed_out,
    packed_in,
    first,
    second,
    third,
    adjoint_ref,
    total_out,
    total_in,
    local_sem,
    result_sem,
    pack_send,
    pack_recv,
    plane_send,
    plane_recv,
    total_send,
    total_recv,
):
    plies, rows, cols = inter_hbm.shape
    cases = strain_hbm.shape[0]
    width = cols + LANES
    mine, tile = lax.axis_index("ply"), lax.axis_index("tile")

    def inside(dp, dt):
        p, t = mine + dp, tile + dt
        return (p >= 0) & (p < groups) & (t >= 0) & (t < tiles)

    has_below, has_above = inside(-1, 0), inside(1, 0)
    has_left, has_right = inside(0, -1), inside(0, 1)

    greeted = [(dp, dt) for dp in (-1, 0, 1) for dt in (-1, 0, 1) if (dp, dt) != (0, 0)]
    greeted += [(dp, 0) for dp in range(1 - groups, groups) if abs(dp) > 1]
    greeted = [(dp, dt) for dp, dt in greeted if abs(dp) < groups]

    locals_ = [
        pltpu.make_async_copy(angle_hbm, angle_ref, local_sem.at[2]),
        pltpu.make_async_copy(case_hbm, case_ref, local_sem.at[3]),
        pltpu.make_async_copy(strain_hbm, strain_ref, local_sem.at[4]),
        pltpu.make_async_copy(
            inter_hbm, inter.at[pl.ds(PAD, plies), :, pl.ds(0, cols)], local_sem.at[0]
        ),
        pltpu.make_async_copy(
            stiff_hbm, stiff.at[pl.ds(PAD, plies), :, pl.ds(0, cols)], local_sem.at[1]
        ),
    ]
    for copy in locals_:
        copy.start()

    barrier = pltpu.get_barrier_semaphore()
    count = jnp.int32(0)
    for dp, dt in greeted:
        ok = inside(dp, dt)
        count = count + ok.astype(jnp.int32)

        @pl.when(ok)
        def _(dp=dp, dt=dt):
            pl.semaphore_signal(
                barrier, inc=1, device_id=(mine + dp, tile + dt), device_id_type=MESH
            )

    for copy in locals_[:2]:
        copy.wait()

    def table(p, carry):
        angle = angle_ref[p]
        cos_sq = jnp.where(angle == 0, 1.0, jnp.where(angle == 3, 0.0, 0.5))
        sin_sq = 1.0 - cos_sq
        mixed = jnp.where(angle == 1, 0.5, jnp.where(angle == 2, -0.5, 0.0))
        values = (
            4.0 * cos_sq + sin_sq,
            4.0 * sin_sq + cos_sq,
            1.5 * mixed,
            0.3 * cos_sq + 0.65 * sin_sq - 0.96 * mixed,
            0.3 * sin_sq + 0.65 * cos_sq + 0.96 * mixed,
            0.48 * (cos_sq - sin_sq) - 0.35 * mixed,
        )
        at = lax.broadcasted_iota(jnp.int32, (8, LANES), 0)
        block = jnp.zeros((8, LANES), jnp.float32)
        for k, value in enumerate(values):
            block = jnp.where(at == k, value, block)
        coef[p + PAD] = block
        return carry

    lax.fori_loop(0, plies, table, 0, unroll=4)

    def plane_copies(dp):
        if dp > 0:
            moves = [
                (inter_hbm.at[pl.ds(plies - PAD, PAD)], inter.at[pl.ds(0, PAD), :, pl.ds(0, cols)]),
                (stiff_hbm.at[pl.ds(plies - HALO, HALO)], stiff.at[pl.ds(1, HALO), :, pl.ds(0, cols)]),
                (coef.at[pl.ds(plies + 1, HALO)], coef.at[pl.ds(1, HALO)]),
            ]
        else:
            moves = [
                (inter_hbm.at[pl.ds(0, HALO)], inter.at[pl.ds(plies + PAD, HALO), :, pl.ds(0, cols)]),
                (stiff_hbm.at[pl.ds(0, HALO)], stiff.at[pl.ds(plies + PAD, HALO), :, pl.ds(0, cols)]),
                (coef.at[pl.ds(PAD, HALO)], coef.at[pl.ds(plies + PAD, HALO)]),
            ]
        side = int(dp > 0)
        return [
            pltpu.make_async_remote_copy(
                src_ref=src,
                dst_ref=dst,
                send_sem=plane_send.at[side, k],
                recv_sem=plane_recv.at[side, k],
                device_id=(mine + dp, tile),
                device_id_type=MESH,
            )
            for k, (src, dst) in enumerate(moves)
        ]

    pl.semaphore_wait(barrier, count)
    for dp in (1, -1):
        if groups > 1:

            @pl.when(inside(dp, 0))
            def _(dp=dp):
                for copy in plane_copies(dp):
                    copy.start()

    lane = lax.broadcasted_iota(jnp.int32, (rows, LANES), 1)
    slot = lane // 4
    locals_[2].wait()
    low = jnp.zeros((rows, LANES), jnp.float32)
    high = jnp.zeros((rows, LANES), jnp.float32)
    for c in range(cases):
        for k in range(3):
            at = c * 3 + k
            plane = strain_ref[case_ref[c], k]
            strain[at, :, 0:cols] = plane
            head, tail = plane[:, :LANES], plane[:, cols - LANES :]
            low = jnp.where(slot == at, pltpu.roll(head, 4 * at, 1), low)
            high = jnp.where(slot == at, pltpu.roll(tail, 4 * at + 4, 1), high)
    packed_out[0, 2] = low
    packed_out[1, 2] = high

    for copy in locals_[3:]:
        copy.wait()

    def pack(p, carry):
        inter_low, inter_high, stiff_low, stiff_high = carry
        here = slot == p
        up, down = 4 * p, 4 * p + 4
        e = p + PAD
        inter_low = jnp.where(here, pltpu.roll(inter[e, :, 0:LANES], up, 1), inter_low)
        inter_high = jnp.where(here, pltpu.roll(inter[e, :, cols - LANES : cols], down, 1), inter_high)
        stiff_low = jnp.where(here, pltpu.roll(stiff[e, :, 0:LANES], up, 1), stiff_low)
        stiff_high = jnp.where(here, pltpu.roll(stiff[e, :, cols - LANES : cols], down, 1), stiff_high)
        return inter_low, inter_high, stiff_low, stiff_high

    zero = jnp.zeros((rows, LANES), jnp.float32)
    inter_low, inter_high, stiff_low, stiff_high = lax.fori_loop(0, plies, pack, (zero,) * 4, unroll=8)
    packed_out[0, 0] = inter_low
    packed_out[1, 0] = inter_high
    packed_out[0, 1] = stiff_low
    packed_out[1, 1] = stiff_high

    def pack_copy(dp, dt):
        depth = 3 if dp == 0 else 2
        group, side = 1 - dp, int(dt < 0)
        return pltpu.make_async_remote_copy(
            src_ref=packed_out.at[1 - side, pl.ds(0, depth)],
            dst_ref=packed_in.at[group, side, pl.ds(0, depth)],
            send_sem=pack_send.at[group, side],
            recv_sem=pack_recv.at[group, side],
            device_id=(mine + dp, tile + dt),
            device_id_type=MESH,
        )

    corners = [(dp, dt) for dp in (0, -1, 1) for dt in (-1, 1) if abs(dp) < groups]
    for dp, dt in corners:

        @pl.when(inside(dp, dt))
        def _(dp=dp, dt=dt):
            pack_copy(dp, dt).start()

    def source_of(e, c, begin, count):
        at = pl.ds(begin * LANES, count * LANES)
        sx, sy, sxy = (strain[3 * c + k, :, at] for k in range(3))
        a, b, g = (wide(coef[e, k : k + 1, :], rows, count) for k in (3, 4, 5))
        return 1.1 + a * sx + b * sy + g * sxy

    full = cols // LANES

    def start_block(e):
        rigid = inter[e, :, 0:cols] + inter[e - 1, :, 0:cols] + stiff[e, :, 0:cols]
        weight = (2.0 / 3.0) / (10.0 + rigid)
        stiff[e, :, 0:cols] = weight
        for c in range(cases):
            first[c, e, :, 0:cols] = weight * source_of(e, c, 0, full)

    def start_pair(i, carry):
        for k in range(2):
            start_block(PAD + 1 + 2 * i + k)
        return carry

    lax.fori_loop(0, (plies - 1) // 2, start_pair, 0)
    if plies % 2 == 0:
        start_block(PAD + plies - 1)

    for group in range(3):
        for side, there in ((0, has_left), (1, has_right)):

            @pl.when(jnp.logical_not(there))
            def _(group=group, side=side):
                packed_in[group, side] = jnp.zeros((3, rows, LANES), jnp.float32)

    @pl.when(jnp.logical_not(has_below))
    def _():
        inter[PAD - 1] = jnp.zeros((rows, width), jnp.float32)
        for c in range(cases):
            for field in (first, second, third):
                field[c, PAD - 1] = jnp.zeros((rows, width), jnp.float32)

    @pl.when(jnp.logical_not(has_above))
    def _():
        for c in range(cases):
            for field in (first, second, third):
                field[c, plies + PAD] = jnp.zeros((rows, width), jnp.float32)

    for dp, dt in corners:

        @pl.when(inside(-dp, -dt))
        def _(dp=dp, dt=dt):
            pack_copy(dp, dt).wait_recv()

    for dp in (1, -1):
        if groups > 1:

            @pl.when(inside(-dp, 0))
            def _(dp=dp):
                for copy in plane_copies(dp):
                    copy.wait_recv()

    upper_half = lane < LANES // 2

    def halo_tile(group, kind, q):
        right = pltpu.roll(packed_in[group, 1, kind], lax.rem(LANES - 4 * q, LANES), 1)
        left = pltpu.roll(packed_in[group, 0, kind], LANES - 4 - 4 * q, 1)
        return jnp.where(upper_half, right, left)

    for at in range(3 * cases):
        strain[at, :, cols:width] = halo_tile(1, 2, jnp.int32(at))

    start_block(PAD)

    numerator = jnp.where(
        upper_half, jnp.where(has_right, 2.0 / 3.0, 0.0), jnp.where(has_left, 2.0 / 3.0, 0.0)
    )

    def start_halo(e, group, q, under):
        over = halo_tile(group, 0, q)
        inter[e, :, cols:width] = over
        weight = numerator / (10.0 + over + under + halo_tile(group, 1, q))
        stiff[e, :, cols:width] = weight
        for c in range(cases):
            first[c, e, :, cols:width] = weight * source_of(e, c, full, 1)
        return over

    @pl.when(has_below)
    def _():
        under = halo_tile(0, 0, jnp.int32(plies - PAD))
        inter[0, :, cols:width] = under

        def below(e, under):
            start_block(e)
            return start_halo(e, 0, plies - PAD + e, under)

        under = lax.fori_loop(1, PAD, below, under)

    under = jnp.where(has_below, inter[PAD - 1, :, cols:width], 0.0)
    under = lax.fori_loop(
        0, plies, lambda p, under: start_halo(p + PAD, 1, p, under), under, unroll=4
    )

    @pl.when(has_above)
    def _():
        def above(q, under):
            start_block(q + plies + PAD)
            return start_halo(q + plies + PAD, 2, q, under)

        lax.fori_loop(0, HALO, above, under)

    half = rows // 2
    row = lax.broadcasted_iota(jnp.int32, (half, width), 0)
    is_last, is_first = row == half - 1, row == 0

    def from_next_row(x):
        a, b = (pltpu.roll(part, half - 1, 0) for part in (x[:half], x[half:]))
        return jnp.concatenate([jnp.where(is_last, b, a), jnp.where(is_last, 0.0, b)], axis=0)

    def from_row_before(x):
        a, b = (pltpu.roll(part, 1, 0) for part in (x[:half], x[half:]))
        return jnp.concatenate([jnp.where(is_first, 0.0, a), jnp.where(is_first, a, b)], axis=0)

    def swept(e, c, field, tables):
        rows_c, cols_c, cross_c, weight, over, under = tables
        v = field[c, e]
        right = pltpu.roll(v, width - 1, 1)
        left = pltpu.roll(v, 1, 1)
        along = rows_c * v
        cross = cross_c * (right - left)
        upper = from_next_row(along + cross)
        lower = from_row_before(along - cross)
        pull = (upper + lower) + cols_c * (right + left)
        pull = pull + (over * field[c, e + 1] + under * field[c, e - 1])
        return (v * (1.0 / 3.0) + first[c, e]) + weight * pull

    def tables_of(e):
        count = width // LANES
        rows_c, cols_c, cross_c = (wide(coef[e, k : k + 1, :], rows, count) for k in range(3))
        return rows_c, cols_c, cross_c, stiff[e], inter[e], inter[e - 1]

    for depth, old, new in ((2, first, second), (1, second, third)):

        def step(e, carry, old=old, new=new):
            tables = tables_of(e)
            for c in range(cases):
                new[c, e] = swept(e, c, old, tables)
            return carry

        @pl.when(has_below)
        def _(depth=depth, step=step):
            lax.fori_loop(PAD - depth, PAD, step, 0)

        @pl.when(has_above)
        def _(depth=depth, step=step):
            lax.fori_loop(plies + PAD, plies + PAD + depth, step, 0)

        lax.fori_loop(PAD, plies + PAD, step, 0, unroll=2)

    share = 1.0 / (plies * groups)

    def last(p, running):
        e = p + PAD
        tables = tables_of(e)
        for c in range(cases):
            value = swept(e, c, third, tables)[:, 0:cols]
            adjoint_ref[c, p] = value
            running = running + value * source_of(e, c, 0, full)
        through_ref[p] = running * share
        pltpu.make_async_copy(
            adjoint_ref.at[:, pl.ds(p, 1)], adjoint_hbm.at[:, pl.ds(p, 1)], result_sem.at[0]
        ).start()
        return running

    running = lax.fori_loop(0, plies, last, jnp.zeros((rows, cols), jnp.float32), unroll=2)
    total_out[...] = running * share

    def total_copy(by):
        return pltpu.make_async_remote_copy(
            src_ref=total_out,
            dst_ref=total_in.at[by - 1],
            send_sem=total_send.at[by - 1],
            recv_sem=total_recv.at[by - 1],
            device_id=(mine + by, tile),
            device_id_type=MESH,
        )

    for by in range(1, groups):

        @pl.when(inside(by, 0))
        def _(by=by):
            total_copy(by).start()

    for dp, dt in corners:

        @pl.when(inside(dp, dt))
        def _(dp=dp, dt=dt):
            pack_copy(dp, dt).wait_send()

    for dp in (1, -1):
        if groups > 1:

            @pl.when(inside(dp, 0))
            def _(dp=dp):
                for copy in plane_copies(dp):
                    copy.wait_send()

    for by in range(1, groups):

        @pl.when(inside(-by, 0))
        def _(by=by):
            total_copy(by).wait_recv()

            def add(p, carry):
                through_ref[p] = through_ref[p] + total_in[by - 1]
                return carry

            lax.fori_loop(0, plies, add, 0, unroll=4)

    for by in range(1, groups):

        @pl.when(inside(by, 0))
        def _(by=by):
            total_copy(by).wait_send()

    pltpu.make_async_copy(adjoint_ref, adjoint_hbm, result_sem.at[0]).wait()


def hand_over(parts, adjoint_in, through_in, adjoint_out, through_out, held, kept, sem, out_sem):
    plies = through_in.shape[0]
    step = plies // parts
    copies = []
    for k in range(parts):
        at = pl.ds(k * step, step)
        for c in range(adjoint_in.shape[0]):
            copies.append((adjoint_in.at[c, at], held.at[c, at], adjoint_out.at[c, at]))
        copies.append((through_in.at[at], kept.at[at], through_out.at[at]))
    inward = [pltpu.make_async_copy(a, b, sem.at[k]) for k, (a, b, _) in enumerate(copies)]
    outward = [pltpu.make_async_copy(b, c, out_sem.at[k]) for k, (_, b, c) in enumerate(copies)]
    for copy in inward:
        copy.start()
    for arriving, leaving in zip(inward, outward):
        arriving.wait()
        leaving.start()
    for copy in outward:
        copy.wait()


def handed_over(adjoint, through):
    parts = 2 if through.shape[0] % 2 == 0 else 1
    hbm = pl.BlockSpec(memory_space=pltpu.HBM)
    return pl.pallas_call(
        functools.partial(hand_over, parts),
        out_shape=tuple(jax.ShapeDtypeStruct(a.shape, a.dtype) for a in (adjoint, through)),
        in_specs=[hbm, hbm],
        out_specs=(hbm, hbm),
        scratch_shapes=[
            pltpu.VMEM(adjoint.shape, jnp.float32),
            pltpu.VMEM(through.shape, jnp.float32),
            pltpu.SemaphoreType.DMA((parts * (adjoint.shape[0] + 1),)),
            pltpu.SemaphoreType.DMA((parts * (adjoint.shape[0] + 1),)),
        ],
        compiler_params=pltpu.CompilerParams(vmem_limit_bytes=56 * 1024 * 1024),
    )(adjoint, through)


def body(groups, tiles, strain, case_ids, angle_ids, stiffening, interface):
    plies, rows, cols = interface.shape
    cases = strain.shape[0]
    ext, width = plies + 2 * PAD, cols + LANES
    vmem = lambda *shape: pltpu.VMEM(shape, jnp.float32)
    dma = pltpu.SemaphoreType.DMA
    others = max(groups - 1, 1)
    adjoint, through = pl.pallas_call(
        functools.partial(kernel, groups, tiles),
        out_shape=(
            jax.ShapeDtypeStruct((cases, plies, rows, cols), jnp.float32),
            jax.ShapeDtypeStruct((plies, rows, cols), jnp.float32),
        ),
        in_specs=[pl.BlockSpec(memory_space=pltpu.HBM)] * 5,
        out_specs=(
            pl.BlockSpec(memory_space=pltpu.HBM),
            pl.BlockSpec(memory_space=pltpu.VMEM),
        ),
        scratch_shapes=[
            pltpu.SMEM(case_ids.shape, jnp.int32),
            pltpu.SMEM(angle_ids.shape, jnp.int32),
            vmem(*strain.shape),
            vmem(ext, rows, width),
            vmem(ext, rows, width),
            vmem(ext, 8, LANES),
            vmem(3 * cases, rows, width),
            vmem(2, 3, rows, LANES),
            vmem(3, 2, 3, rows, LANES),
            vmem(cases, ext, rows, width),
            vmem(cases, ext, rows, width),
            vmem(cases, ext, rows, width),
            vmem(cases, plies, rows, cols),
            vmem(rows, cols),
            vmem(others, rows, cols),
            dma((5,)),
            dma((1,)),
            dma((3, 2)),
            dma((3, 2)),
            dma((2, 3)),
            dma((2, 3)),
            dma((others,)),
            dma((others,)),
        ],
        compiler_params=pltpu.CompilerParams(
            collective_id=0, has_side_effects=True, vmem_limit_bytes=56 * 1024 * 1024
        ),
    )(case_ids, angle_ids, strain, stiffening, interface)
    return tuple(handed_over(adjoint, through))


def solution(mesh):
    return jax.shard_map(
        functools.partial(body, mesh.shape["ply"], mesh.shape["tile"]),
        mesh=mesh,
        in_specs=(
            P(None, None, None, "tile"),
            P(),
            P("ply"),
            P("ply", None, "tile"),
            P("ply", None, "tile"),
        ),
        out_specs=(P(None, "ply", None, "tile"), P("ply", None, "tile")),
        check_vma=False,
    )
```
